32 devices in a mesh: dp: 4 (over z), expert: 8 (over y, x, core).
Axes of the slice: x: 2, y: 2, z: 4, core: 2. Of those that a mesh axis runs over, the one named last changes fastest.
Arguments:
- tokens: bfloat16 [4096, 3584], P(('dp', 'expert')), may hold values from -6 to 6
- cotangent: bfloat16 [4096, 3584], P(('dp', 'expert')), may hold values from -6 to 6
- routes: int32 [4096, 1], P(('dp', 'expert')), may hold values from 0 to 7; in each aligned block of 128 rows (0 to 127, 128 to 255, ...) at most 20 rows name the same one
- gates: float32 [4096, 1], P(('dp', 'expert')), may hold values from 0.1 to 1
- w_gate_up: bfloat16 [2, 3584, 8192], P(None, 'dp', 'expert'), may hold values from -0.09375 to 0.09375
- w_down: bfloat16 [8192, 3584], P('expert', 'dp'), may hold values from -0.1875 to 0.1875
- m_gate_up: float32 [2, 3584, 8192], P(None, 'dp', 'expert'), may hold values from -2 to 2
- v_gate_up: float32 [2, 3584, 8192], P(None, 'dp', 'expert'), may hold values from 0.01 to 1
- m_down: float32 [8192, 3584], P('expert', 'dp'), may hold values from -2 to 2
- v_down: float32 [8192, 3584], P('expert', 'dp'), may hold values from 0.01 to 1
Outputs:
- outputs: bfloat16 [4096, 3584], P(('dp', 'expert'))
- input_grads: bfloat16 [4096, 3584], P(('dp', 'expert'))
- new_w_gate_up: bfloat16 [2, 3584, 8192], P(None, 'dp', 'expert')
- new_m_gate_up: float32 [2, 3584, 8192], P(None, 'dp', 'expert')
- new_v_gate_up: float32 [2, 3584, 8192], P(None, 'dp', 'expert')
- new_w_down: bfloat16 [8192, 3584], P('expert', 'dp')
- new_m_down: float32 [8192, 3584], P('expert', 'dp')
- new_v_down: float32 [8192, 3584], P('expert', 'dp')
The draws below stay inside these ranges and needn't reach their ends.
Inputs may be any that keep to these rules, and one draw needn't show every extreme that they name: `routes`: among the rows of one device, no expert is named more than 20 times, and one expert is named exactly 20 times in some devices' rows.
All inputs are finite; a program needn't handle non-finite values.
Results may differ from the reference program's by a relative error of at most 0.014.
Values may be sent and summed in bfloat16 or wider, within the bound.
A program may use at most 192 MiB of HBM per device.

```python
import math
import jax
import jax.numpy as jnp
import numpy as np
from jax import lax

D = 3584
FF = 1024
EXPERTS = 8
ROUTED = 1
TOK_DEV = 128
CAPACITY = 20
TOKENS = 4096
N_DP = 4
N_EXPERT = 8


def level_of(own_key, extent, pieces, least, largest):
    level = 1.0
    for position, shards_of in pieces:
        steps = jax.random.uniform(jax.random.fold_in(jax.random.fold_in(own_key, 6), position), (shards_of,), jnp.float32, least / len(pieces), largest / len(pieces))
        level = level * jnp.repeat(jnp.exp(steps), extent[position] // shards_of).reshape((-1,) + (1,) * (len(extent) - 1 - position))
    return level


def deal_out(key, own, number, rows, amount, top, bound, slope):
    order = jax.random.permutation(key, amount)
    crowded, ordinary = portions_of(amount, rows * top, bound, slope, True), portions_of(amount, rows * top, bound, slope, False)
    places = jnp.arange(amount)

    def named(lengths, rotation):
        used = int((lengths > 0).sum())
        fixed = max(1, used // 4)
        passed = fixed + (places - fixed + rotation * (used - fixed)) % max(1, amount - fixed)
        return jnp.zeros((amount,), jnp.int32).at[order[jnp.where(places < fixed, places, passed)]].set(jnp.asarray(lengths, jnp.int32))

    lengths = jnp.where(number % 4 == 0, named(crowded, number // 4), named(ordinary, number - number // 4 - 1))
    mixed = jax.random.permutation(jax.random.fold_in(own, 3), amount)
    giver, taker = mixed[0:amount // 2 * 2:2], mixed[1:amount // 2 * 2:2]
    slack = jnp.minimum(lengths[giver] - 1, bound - lengths[taker]) // 2
    slack = jnp.where((giver == order[0]) | (taker == order[0]) | (lengths[taker] == 0), 0, jnp.maximum(slack, 0))
    passed = jax.random.randint(jax.random.fold_in(own, 4), (amount // 2,), 0, 1 << 20) % (slack + 1)
    lengths = lengths.at[giver].add(-passed).at[taker].add(passed)
    items = jnp.searchsorted(jnp.cumsum(lengths), jnp.arange(rows * top), side="right").astype(jnp.int32)
    listing = items.reshape(top, rows).T
    listing = listing[jax.random.permutation(jax.random.fold_in(own, 1), rows)]
    rotation = jax.random.randint(jax.random.fold_in(own, 2), (rows, 1), 0, top)
    return jnp.take_along_axis(listing, (jnp.arange(top)[None, :] + rotation) % top, axis=1)


def portions_of(count, total, limit, slope, full):
    portions = [(1 << 20) // math.isqrt(rank ** slope) + 1 for rank in range(1, count + 1)]
    largest = limit if full else min(limit, max(-(-total // count), total * portions[0] // sum(portions)))
    least = 1 if total - largest >= count - 1 else 0
    counts, spare = [largest] + [least] * (count - 1), total - largest - least * (count - 1)
    while spare > 0:
        movable = [i for i in range(1, count) if counts[i] < largest] or [i for i in range(1, count) if counts[i] < limit]
        pool, budget = sum([portions[i] for i in movable]), spare
        for i in movable:
            addition = min(limit - counts[i], max(1, budget * portions[i] // pool), spare)
            counts[i] = counts[i] + addition
            spare = spare - addition
    return np.array(counts)


def centred(key, dims, deviation, reach, cuts=(), kind=jnp.bfloat16):
    factor_of = level_of(key, dims, cuts, -0.22, 0.18) if cuts else 1.0
    array = jax.random.normal(key, dims, jnp.float32) * deviation * factor_of
    return jnp.minimum(jnp.maximum(array, -reach), reach).astype(kind)


def setup_inputs(seed: int = 0) -> dict:
    keys = jax.random.split(jax.random.key(seed), 11)
    tokens = centred(keys[0], (TOKENS, D), 1.0, 6.0, ((0, 32),))
    cotangent = centred(keys[1], (TOKENS, D), 1.0, 6.0, ((0, 32),))
    routes_keys = jax.random.split(jax.random.fold_in(keys[2], 1), TOKENS // TOK_DEV)
    routes_turns = jax.random.permutation(jax.random.fold_in(keys[2], 3), TOKENS // TOK_DEV)
    routes = jax.vmap(lambda own, number: deal_out(jax.random.fold_in(keys[2], 2), own, number, TOK_DEV, EXPERTS, ROUTED, CAPACITY, 1))(routes_keys, routes_turns).reshape((TOKENS, ROUTED))
    gates = jnp.clip(0.1 + 0.9 * jax.random.uniform(keys[3], (TOKENS, ROUTED), jnp.float32) ** level_of(keys[3], (TOKENS, ROUTED), ((0, 32),), -0.2, 0.2), 0.1, 1.0)
    w_gate_up = centred(keys[4], (2, D, EXPERTS * FF), D ** -0.5, 0.09375, ((1, 4), (2, 8)))
    w_down = centred(keys[5], (EXPERTS * FF, D), FF ** -0.5, 0.1875, ((0, 8), (1, 4)))
    m_gate_up = centred(keys[6], (2, D, EXPERTS * FF), 0.3, 2.0, ((1, 4), (2, 8)), jnp.float32)
    v_gate_up = jnp.clip(jnp.exp(math.log(1.0) - 4.6051702 * jax.random.uniform(keys[7], (2, D, EXPERTS * FF), jnp.float32) ** level_of(keys[7], (2, D, EXPERTS * FF), ((1, 4), (2, 8)), -0.2, 0.2)), 0.01, 1.0)
    m_down = centred(keys[8], (EXPERTS * FF, D), 0.3, 2.0, ((0, 8), (1, 4)), jnp.float32)
    v_down = jnp.clip(jnp.exp(math.log(1.0) - 4.6051702 * jax.random.uniform(keys[9], (EXPERTS * FF, D), jnp.float32) ** level_of(keys[9], (EXPERTS * FF, D), ((0, 8), (1, 4)), -0.2, 0.2)), 0.01, 1.0)
    return dict(tokens=tokens, cotangent=cotangent, routes=routes, gates=gates, w_gate_up=w_gate_up, w_down=w_down, m_gate_up=m_gate_up, v_gate_up=v_gate_up, m_down=m_down, v_down=v_down)


first_decay = 0.9
second_decay = 0.95
first_correction = 1.0 - 0.9 ** 50 * 0.9 ** 50
second_correction = 1.0 - 0.95 ** 50 * 0.95 ** 50
learn_rate = 0.01
adam_epsilon = 1e-08

def round_trip(value):
    return lax.optimization_barrier(value.astype(jnp.bfloat16)).astype(jnp.float32)

def slot_positions(flat_routes):
    experts_iota = jnp.arange(EXPERTS, dtype=jnp.int32)
    onehot = (flat_routes[:, None] == experts_iota[None, :]).astype(jnp.int32)
    before = jnp.cumsum(onehot, axis=0) - onehot
    slots = lax.optimization_barrier(jnp.sum(before * onehot, axis=1))
    return (flat_routes * CAPACITY + slots).astype(jnp.int32)

def adam_update(weight, moment, second, grad_sum):
    grad = grad_sum * (TOKENS * ROUTED / EXPERTS) ** (-0.5)
    moment_new = first_decay * moment + (1.0 - first_decay) * grad
    second_new = second_decay * second + (1.0 - second_decay) * grad * grad
    update = moment_new / first_correction / (jnp.sqrt(second_new / second_correction) + adam_epsilon)
    weight_new = (weight.astype(jnp.float32) - learn_rate * update).astype(jnp.bfloat16)
    return (weight_new, moment_new, second_new)

def reference(tokens, cotangent, routes, gates, w_gate_up, w_down, m_gate_up, v_gate_up, m_down, v_down):
    group = N_EXPERT // EXPERTS
    block_width = FF // group
    per_device = TOK_DEV * ROUTED
    tok = tokens.reshape(N_DP, N_EXPERT, TOK_DEV, D)
    cot = cotangent.reshape(N_DP, N_EXPERT, TOK_DEV, D)
    flat_routes = routes.reshape(N_DP, N_EXPERT, per_device)
    gts = gates.reshape(N_DP, N_EXPERT, TOK_DEV, ROUTED)
    places = jax.vmap(jax.vmap(slot_positions))(flat_routes)
    gate_up = w_gate_up.reshape(2, D, EXPERTS, FF).transpose(2, 0, 1, 3)
    down = w_down.reshape(EXPERTS, FF, D)

    def pack(rows, where):
        buffer = jnp.zeros((EXPERTS * CAPACITY, D), jnp.bfloat16).at[where].set(rows)
        return buffer.reshape(EXPERTS, CAPACITY, D)

    def expert_pass(items):
        inputs, grads_in, weights_up, weights_down = items
        pre = jnp.einsum('rc,gcf->grf', inputs.astype(jnp.float32), weights_up.astype(jnp.float32))
        act_in = pre[0]
        linear = pre[1]
        sig = jax.nn.sigmoid(act_in)
        hidden = (act_in * sig * linear).astype(jnp.bfloat16)
        d_hidden = jnp.dot(grads_in, weights_down.T, preferred_element_type=jnp.float32)
        d_act = (d_hidden * linear * sig * (1.0 + act_in * (1.0 - sig))).astype(jnp.bfloat16)
        d_lin = (d_hidden * act_in * sig).astype(jnp.bfloat16)
        d_pre = jnp.stack([d_act, d_lin])
        outs_sum = jnp.zeros((inputs.shape[0], D), jnp.float32)
        ins_sum = jnp.zeros((inputs.shape[0], D), jnp.float32)
        for part in range(group):
            low = part * block_width
            high = low + block_width
            outs_sum = outs_sum + round_trip(jnp.dot(hidden[:, low:high], weights_down[low:high], preferred_element_type=jnp.float32))
            ins_sum = ins_sum + round_trip(jnp.einsum('grf,gcf->rc', d_pre[:, :, low:high].astype(jnp.float32), weights_up[:, :, low:high].astype(jnp.float32)))
        grad_up = jnp.einsum('rc,grf->gcf', inputs.astype(jnp.float32), d_pre.astype(jnp.float32))
        grad_down = jnp.dot(hidden.T, grads_in, preferred_element_type=jnp.float32)
        return (outs_sum, ins_sum, round_trip(grad_up), round_trip(grad_down))

    def data_row(carry, row):
        tok_d, cot_d, place_d, gate_d = row
        token_rows = jnp.repeat(tok_d, ROUTED, axis=1)
        gate_flat = gate_d.reshape(N_EXPERT, per_device)
        cot_rows = (gate_flat[..., None] * jnp.repeat(cot_d, ROUTED, axis=1).astype(jnp.float32)).astype(jnp.bfloat16)
        send_x = jax.vmap(pack)(token_rows, place_d)
        send_y = jax.vmap(pack)(cot_rows, place_d)
        inputs = send_x.transpose(1, 0, 2, 3).reshape(EXPERTS, N_EXPERT * CAPACITY, D)
        grads_in = send_y.transpose(1, 0, 2, 3).reshape(EXPERTS, N_EXPERT * CAPACITY, D)
        outs, ins, g_up, g_down = lax.map(expert_pass, (inputs, grads_in, gate_up, down))
        outs_src = outs.reshape(EXPERTS, N_EXPERT, CAPACITY, D).transpose(1, 0, 2, 3).reshape(N_EXPERT, EXPERTS * CAPACITY, D)
        ins_src = ins.reshape(EXPERTS, N_EXPERT, CAPACITY, D).transpose(1, 0, 2, 3).reshape(N_EXPERT, EXPERTS * CAPACITY, D)
        picked_out = jax.vmap(lambda source, where: source[where])(outs_src, place_d).reshape(N_EXPERT, TOK_DEV, ROUTED, D)
        picked_in = jax.vmap(lambda source, where: source[where])(ins_src, place_d).reshape(N_EXPERT, TOK_DEV, ROUTED, D)
        row_out = lax.optimization_barrier(jnp.sum(gate_d[..., None] * picked_out, axis=2)).astype(jnp.bfloat16)
        row_in = lax.optimization_barrier(jnp.sum(picked_in, axis=2)).astype(jnp.bfloat16)
        return ((carry[0] + g_up, carry[1] + g_down), (row_out, row_in))
    start = (jnp.zeros((EXPERTS, 2, D, FF), jnp.float32), jnp.zeros((EXPERTS, FF, D), jnp.float32))
    sums, rows_out = lax.scan(data_row, start, (tok, cot, places, gts))
    sum_up = sums[0].transpose(1, 2, 0, 3).reshape(2, D, EXPERTS * FF)
    sum_down = sums[1].reshape(EXPERTS * FF, D)
    outputs = rows_out[0].reshape(TOKENS, D)
    input_grads = rows_out[1].reshape(TOKENS, D)
    new_wu, new_mu, new_vu = adam_update(w_gate_up, m_gate_up, v_gate_up, sum_up)
    new_wd, new_md, new_vd = adam_update(w_down, m_down, v_down, sum_down)
    return (outputs, input_grads, new_wu, new_mu, new_vu, new_wd, new_md, new_vd)
```

```python
import functools

import jax
import jax.numpy as jnp
from jax import lax
from jax.experimental import pallas as pl
from jax.experimental.pallas import tpu as pltpu
from jax.sharding import PartitionSpec as P

EXPERTS = 8
CAPACITY = 20
BOTH = ("dp", "expert")

first_decay = 0.9
second_decay = 0.95
first_correction = 1.0 - 0.9**50 * 0.9**50
second_correction = 1.0 - 0.95**50 * 0.95**50
learn_rate = 0.01
adam_epsilon = 1e-08
f32, bf16 = jnp.float32, jnp.bfloat16


def selections(routes, group):
    tok, topk = routes.shape
    pairs = tok * topk
    onehot = (routes.reshape(-1)[:, None] == jnp.arange(EXPERTS, dtype=jnp.int32)).astype(f32)
    earlier = (jnp.arange(pairs)[:, None] > jnp.arange(pairs)[None, :]).astype(f32)
    before = jnp.dot(earlier, onehot, preferred_element_type=f32)
    slot = jnp.sum(before * onehot, axis=1)
    at_slot = (slot[:, None] == jnp.arange(CAPACITY, dtype=f32)).astype(f32)
    sel = onehot[:, :, None, None] * at_slot[:, None, None, :]
    sel = jnp.broadcast_to(sel, (pairs, EXPERTS, group, CAPACITY))
    sel = sel.reshape(tok, topk, EXPERTS * group * CAPACITY).astype(bf16)
    return [sel[:, k] for k in range(topk)]


def adam_body(scale, a_ref, b_ref, w_ref, m_ref, v_ref, nw_ref, nm_ref, nv_ref):
    total = lax.dot_general(
        a_ref[...], b_ref[...], (((0,), (0,)), ((), ())), preferred_element_type=f32
    )
    grad = total * scale
    moment = first_decay * m_ref[...] + (1.0 - first_decay) * grad
    second = second_decay * v_ref[...] + (1.0 - second_decay) * grad * grad
    update = moment / first_correction / (jnp.sqrt(second / second_correction) + adam_epsilon)
    nw_ref[...] = (w_ref[...].astype(f32) - learn_rate * update).astype(bf16)
    nm_ref[...] = moment
    nv_ref[...] = second


def grad_adam(a, b, w, m, v, scale):
    rows, width = a.shape
    parts, _, cols = b.shape
    tile = 128 if width % 128 == 0 else width
    state = pl.BlockSpec((None, tile, cols), lambda g, i: (g, i, 0))
    size = parts * width * cols
    return pl.pallas_call(
        functools.partial(adam_body, scale),
        grid=(parts, width // tile),
        in_specs=[
            pl.BlockSpec((rows, tile), lambda g, i: (0, i)),
            pl.BlockSpec((None, rows, cols), lambda g, i: (g, 0, 0)),
            state,
            state,
            state,
        ],
        out_specs=[state, state, state],
        out_shape=[
            jax.ShapeDtypeStruct(w.shape, bf16),
            jax.ShapeDtypeStruct(m.shape, f32),
            jax.ShapeDtypeStruct(v.shape, f32),
        ],
        compiler_params=pltpu.CompilerParams(vmem_limit_bytes=48 * 2**20),
        cost_estimate=pl.CostEstimate(
            flops=2 * rows * size, bytes_accessed=20 * size, transcendentals=2 * size
        ),
        name="grad_adam",
    )(a, b, w, m, v)


def shards(
    tokens, cotangent, routes, gates, w_gate_up, w_down, m_gate_up, v_gate_up, m_down, v_down
):
    n_expert = lax.axis_size("expert")
    n_data = lax.axis_size("dp")
    group = n_expert // EXPERTS
    tok, width = tokens.shape
    topk = routes.shape[1]
    block = width // n_data
    rows = n_data * n_expert * CAPACITY
    sels = selections(routes, group)

    def dispatch(per_choice):
        packed = sum(
            lax.dot_general(s, r, (((0,), (0,)), ((), ())), preferred_element_type=f32)
            for s, r in zip(sels, per_choice)
        ).astype(bf16)
        packed = packed.reshape(n_expert, CAPACITY, n_data, block).transpose(2, 0, 1, 3)
        packed = packed.reshape(n_data * n_expert, CAPACITY, block)
        got = lax.all_to_all(packed, BOTH, split_axis=0, concat_axis=0, tiled=True)
        return got.reshape(rows, block)

    def collect(part):
        part = part.reshape(n_data * n_expert, CAPACITY, block)
        back = lax.all_to_all(part, BOTH, split_axis=0, concat_axis=0, tiled=True)
        back = back.reshape(n_data, n_expert * CAPACITY, block)
        return [
            jnp.einsum("tp,dpc->tdc", s, back, preferred_element_type=f32).reshape(tok, width)
            for s in sels
        ]

    inputs = dispatch([tokens] * topk)
    cot = cotangent.astype(f32)
    grads_in = dispatch([(gates[:, k, None] * cot).astype(bf16) for k in range(topk)])

    pre = jnp.einsum("rc,gcf->rgf", inputs, w_gate_up, preferred_element_type=f32)
    hid = w_gate_up.shape[2]
    pre = lax.psum_scatter(
        pre.astype(bf16).reshape(rows, 2 * hid), "dp", scatter_dimension=0, tiled=True
    ).astype(f32)
    d_hidden = lax.dot_general(
        grads_in, w_down, (((1,), (1,)), ((), ())), preferred_element_type=f32
    )
    d_hidden = lax.psum_scatter(
        d_hidden.astype(bf16), "dp", scatter_dimension=0, tiled=True
    ).astype(f32)
    act_in, linear = pre[:, :hid], pre[:, hid:]
    sig = jax.nn.sigmoid(act_in)
    hidden = (act_in * sig * linear).astype(bf16)
    d_act = (d_hidden * linear * sig * (1.0 + act_in * (1.0 - sig))).astype(bf16)
    d_lin = (d_hidden * act_in * sig).astype(bf16)
    hidden = lax.all_gather(hidden, "dp", axis=0, tiled=True)
    d_pre = lax.all_gather(jnp.stack([d_act, d_lin]), "dp", axis=1, tiled=True)

    out_part = jnp.dot(hidden, w_down, preferred_element_type=f32).astype(bf16)
    outs = collect(out_part)
    outputs = sum(gates[:, k, None] * outs[k] for k in range(topk)).astype(bf16)
    in_part = jnp.einsum("grf,gcf->rc", d_pre, w_gate_up, preferred_element_type=f32).astype(bf16)
    input_grads = sum(collect(in_part)).astype(bf16)

    scale = (tok * n_data * n_expert * topk / EXPERTS) ** (-0.5)
    new_wd, new_md, new_vd = (
        x[0]
        for x in grad_adam(
            hidden, grads_in[None], w_down[None], m_down[None], v_down[None], scale
        )
    )
    new_wu, new_mu, new_vu = grad_adam(inputs, d_pre, w_gate_up, m_gate_up, v_gate_up, scale)
    return (outputs, input_grads, new_wu, new_mu, new_vu, new_wd, new_md, new_vd)


def solution(mesh):
    rows = P(BOTH, None)
    up, down = P(None, "dp", "expert"), P("expert", "dp")
    return jax.shard_map(
        shards,
        mesh=mesh,
        in_specs=(rows, rows, rows, rows, up, down, up, up, down, down),
        out_specs=(rows, rows, up, up, up, down, down, down),
        check_vma=False,
    )
```

```python
import functools

import jax
import jax.numpy as jnp
from jax import lax
from jax.experimental import pallas as pl
from jax.experimental.pallas import tpu as pltpu
from jax.sharding import PartitionSpec as P

EXPERTS = 8
CAPACITY = 20
BOTH = ("dp", "expert")

first_decay = 0.9
second_decay = 0.95
first_correction = 1.0 - 0.9**50 * 0.9**50
second_correction = 1.0 - 0.95**50 * 0.95**50
learn_rate = 0.01
adam_epsilon = 1e-08
f32, bf16 = jnp.float32, jnp.bfloat16


def selections(routes, group):
    tok, topk = routes.shape
    pairs = tok * topk
    onehot = (routes.reshape(-1)[:, None] == jnp.arange(EXPERTS, dtype=jnp.int32)).astype(f32)
    earlier = (jnp.arange(pairs)[:, None] > jnp.arange(pairs)[None, :]).astype(f32)
    before = jnp.dot(earlier, onehot, preferred_element_type=f32)
    slot = jnp.sum(before * onehot, axis=1)
    at_slot = (slot[:, None] == jnp.arange(CAPACITY, dtype=f32)).astype(f32)
    sel = onehot[:, :, None, None] * at_slot[:, None, None, :]
    sel = jnp.broadcast_to(sel, (pairs, EXPERTS, group, CAPACITY))
    sel = sel.reshape(tok, topk, EXPERTS * group * CAPACITY).astype(bf16)
    return [sel[:, k] for k in range(topk)]


def adam_body(scale, a_ref, b_ref, w_ref, m_ref, v_ref, nw_ref, nm_ref, nv_ref):
    total = lax.dot_general(
        a_ref[...], b_ref[...], (((0,), (0,)), ((), ())), preferred_element_type=f32
    )
    grad = total * scale
    moment = first_decay * m_ref[...] + (1.0 - first_decay) * grad
    second = second_decay * v_ref[...] + (1.0 - second_decay) * grad * grad
    update = moment / first_correction / (jnp.sqrt(second / second_correction) + adam_epsilon)
    nw_ref[...] = (w_ref[...].astype(f32) - learn_rate * update).astype(bf16)
    nm_ref[...] = moment
    nv_ref[...] = second


def grad_adam(a, b, first, w, m, v, scale):
    rows = a.shape[0]
    parts, width, cols = w.shape
    tile = 128 if width % 128 == 0 else width
    state = pl.BlockSpec((None, tile, cols), lambda g, i: (g, i, 0))
    size = parts * width * cols
    return pl.pallas_call(
        functools.partial(adam_body, scale),
        grid=(parts, width // tile),
        in_specs=[
            pl.BlockSpec((rows, tile), lambda g, i: (0, i)),
            pl.BlockSpec((rows, cols), lambda g, i: (0, first + g)),
            state,
            state,
            state,
        ],
        out_specs=[state, state, state],
        out_shape=[
            jax.ShapeDtypeStruct(w.shape, bf16),
            jax.ShapeDtypeStruct(m.shape, f32),
            jax.ShapeDtypeStruct(v.shape, f32),
        ],
        compiler_params=pltpu.CompilerParams(vmem_limit_bytes=48 * 2**20),
        cost_estimate=pl.CostEstimate(
            flops=2 * rows * size, bytes_accessed=20 * size, transcendentals=2 * size
        ),
        name="grad_adam",
    )(a, b, w, m, v)


SKEW = 2


def line_body(n, chunk, count, ab_ref, g_ref, out_ref, sums, got, send, recv):
    d = lax.axis_index("dp")
    last = n - 1
    hid = g_ref.shape[1]
    half = chunk * count
    has_low, has_high = d > 0, d < last

    barrier = pltpu.get_barrier_semaphore()
    for present, peer in ((has_low, d - 1), (has_high, d + 1)):

        @pl.when(present)
        def _():
            pl.semaphore_signal(
                barrier, inc=1, device_id={"dp": peer}, device_id_type=pl.DeviceIdType.MESH
            )

    pl.semaphore_wait(barrier, has_low.astype(jnp.int32) + has_high.astype(jnp.int32))

    peers = (d + 1, d - 1)
    starts = (d == 0, d == last)
    ends = (d == last, d == 0)

    def rows_of(w, c):
        return pl.ds(pl.multiple_of(w * half + c * chunk, 16), chunk)

    def sum_copy(w, c):
        return pltpu.make_async_remote_copy(
            src_ref=sums.at[rows_of(w, c), :],
            dst_ref=got.at[rows_of(w, c), :],
            send_sem=send.at[w, c],
            recv_sem=recv.at[w, c],
            device_id={"dp": peers[w]},
            device_id_type=pl.DeviceIdType.MESH,
        )

    def result_copy(w, c):
        return pltpu.make_async_remote_copy(
            src_ref=out_ref.at[rows_of(w, c), :],
            dst_ref=out_ref.at[rows_of(w, c), :],
            send_sem=send.at[2 + w, c],
            recv_sem=recv.at[2 + w, c],
            device_id={"dp": peers[1 - w]},
            device_id_type=pl.DeviceIdType.MESH,
        )

    def step(s, carry):
        for w in range(2):
            place = d if w == 0 else last - d
            c = s - SKEW * place

            @pl.when((c >= 0) & (c < count))
            def _():
                rows = rows_of(w, c)

                @pl.when(starts[w])
                def _():
                    sums[rows, : 2 * hid] = ab_ref[rows, :]
                    sums[rows, 2 * hid :] = g_ref[rows, :]
                    sum_copy(w, c).start()

                @pl.when(jnp.logical_not(starts[w]))
                def _():
                    sum_copy(w, c).wait_recv()

                @pl.when(jnp.logical_not(starts[w] | ends[w]))
                def _():
                    sums[rows, : 2 * hid] = (
                        got[rows, : 2 * hid].astype(f32) + ab_ref[rows, :].astype(f32)
                    ).astype(bf16)
                    sums[rows, 2 * hid :] = (
                        got[rows, 2 * hid :].astype(f32) + g_ref[rows, :].astype(f32)
                    ).astype(bf16)
                    sum_copy(w, c).start()

                @pl.when(ends[w])
                def _():
                    a = got[rows, :hid].astype(f32) + ab_ref[rows, :hid].astype(f32)
                    b = got[rows, hid : 2 * hid].astype(f32) + ab_ref[rows, hid:].astype(f32)
                    g = got[rows, 2 * hid :].astype(f32) + g_ref[rows, :].astype(f32)
                    sig = jax.nn.sigmoid(a)
                    out_ref[rows, :hid] = (a * sig * b).astype(bf16)
                    out_ref[rows, hid : 2 * hid] = (
                        g * b * sig * (1.0 + a * (1.0 - sig))
                    ).astype(bf16)
                    out_ref[rows, 2 * hid :] = (g * a * sig).astype(bf16)
                    result_copy(w, c).start()

        for w in range(2):
            place = d if w == 0 else last - d
            c = s - SKEW * (2 * last - place)

            @pl.when((c >= 0) & (c < count) & jnp.logical_not(ends[w]))
            def _():
                result_copy(w, c).wait_recv()

                @pl.when(jnp.logical_not(starts[w]))
                def _():
                    result_copy(w, c).start()

        return carry

    lax.fori_loop(0, count + 2 * SKEW * last, step, 0)

    def drain(c, carry):
        for w in range(2):

            @pl.when(jnp.logical_not(ends[w]))
            def _():
                sum_copy(w, c).wait_send()

            @pl.when(jnp.logical_not(starts[w]))
            def _():
                result_copy(w, c).wait_send()

        return carry

    lax.fori_loop(0, count, drain, 0)


def line_activations(ab, g, n):
    rows, hid = g.shape
    half = rows // 2
    count = max(c for c in range(1, 21) if half % (16 * c) == 0)
    whole = pl.BlockSpec(memory_space=pltpu.VMEM)
    full = jax.ShapeDtypeStruct((rows, 3 * hid), bf16)
    return pl.pallas_call(
        functools.partial(line_body, n, half // count, count),
        out_shape=full,
        in_specs=[whole, whole],
        out_specs=whole,
        scratch_shapes=[
            pltpu.VMEM(full.shape, bf16),
            pltpu.VMEM(full.shape, bf16),
            pltpu.SemaphoreType.DMA((4, count)),
            pltpu.SemaphoreType.DMA((4, count)),
        ],
        compiler_params=pltpu.CompilerParams(
            collective_id=0, has_side_effects=True, vmem_limit_bytes=56 * 2**20
        ),
        cost_estimate=pl.CostEstimate(
            flops=30 * rows * hid, bytes_accessed=12 * rows * hid, transcendentals=rows * hid
        ),
        name="line_activations",
    )(ab, g)


def shards(
    tokens, cotangent, routes, gates, w_gate_up, w_down, m_gate_up, v_gate_up, m_down, v_down
):
    n_expert = lax.axis_size("expert")
    n_data = lax.axis_size("dp")
    group = n_expert // EXPERTS
    tok, width = tokens.shape
    topk = routes.shape[1]
    block = width // n_data
    rows = n_data * n_expert * CAPACITY
    sels = selections(routes, group)

    def dispatch(per_choice):
        packed = sum(
            lax.dot_general(s, r, (((0,), (0,)), ((), ())), preferred_element_type=f32)
            for s, r in zip(sels, per_choice)
        ).astype(bf16)
        packed = packed.reshape(n_expert, CAPACITY, n_data, block).transpose(2, 0, 1, 3)
        packed = packed.reshape(n_data * n_expert, CAPACITY, block)
        got = lax.all_to_all(packed, BOTH, split_axis=0, concat_axis=0, tiled=True)
        return got.reshape(rows, block)

    def collect(part):
        part = part.reshape(n_data * n_expert, CAPACITY, block)
        back = lax.all_to_all(part, BOTH, split_axis=0, concat_axis=0, tiled=True)
        back = back.reshape(n_data, n_expert * CAPACITY, block)
        return [
            jnp.einsum("tp,dpc->tdc", s, back, preferred_element_type=f32).reshape(tok, width)
            for s in sels
        ]

    inputs = dispatch([tokens] * topk)
    cot = cotangent.astype(f32)
    grads_in = dispatch([(gates[:, k, None] * cot).astype(bf16) for k in range(topk)])

    hid = w_gate_up.shape[2]
    pre = jnp.einsum("rc,gcf->rgf", inputs, w_gate_up, preferred_element_type=f32)
    pre = pre.astype(bf16).reshape(rows, 2 * hid)
    d_hidden = lax.dot_general(
        grads_in, w_down, (((1,), (1,)), ((), ())), preferred_element_type=f32
    ).astype(bf16)
    acts = line_activations(pre, d_hidden, n_data)

    out_part = jnp.dot(acts[:, :hid], w_down, preferred_element_type=f32).astype(bf16)
    outs = collect(out_part)
    outputs = sum(gates[:, k, None] * outs[k] for k in range(topk)).astype(bf16)
    across = (((1,), (1,)), ((), ()))
    in_part = (
        lax.dot_general(acts[:, hid : 2 * hid], w_gate_up[0], across, preferred_element_type=f32)
        + lax.dot_general(acts[:, 2 * hid :], w_gate_up[1], across, preferred_element_type=f32)
    ).astype(bf16)
    input_grads = sum(collect(in_part)).astype(bf16)

    scale = (tok * n_data * n_expert * topk / EXPERTS) ** (-0.5)
    new_wd, new_md, new_vd = (
        x[0]
        for x in grad_adam(
            acts, grads_in, 0, w_down[None], m_down[None], v_down[None], scale
        )
    )
    new_wu, new_mu, new_vu = grad_adam(inputs, acts, 1, w_gate_up, m_gate_up, v_gate_up, scale)
    return (outputs, input_grads, new_wu, new_mu, new_vu, new_wd, new_md, new_vd)


def solution(mesh):
    rows = P(BOTH, None)
    up, down = P(None, "dp", "expert"), P("expert", "dp")
    return jax.shard_map(
        shards,
        mesh=mesh,
        in_specs=(rows, rows, rows, rows, up, down, up, up, down, down),
        out_specs=(rows, rows, up, up, up, down, down, down),
        check_vma=False,
    )
```

```python
import functools

import jax
import jax.numpy as jnp
from jax import lax
from jax.experimental import pallas as pl
from jax.experimental.pallas import tpu as pltpu
from jax.sharding import PartitionSpec as P

EXPERTS = 8
CAPACITY = 20
BOTH = ("dp", "expert")

first_decay = 0.9
second_decay = 0.95
first_correction = 1.0 - 0.9**50 * 0.9**50
second_correction = 1.0 - 0.95**50 * 0.95**50
learn_rate = 0.01
adam_epsilon = 1e-08
f32, bf16 = jnp.float32, jnp.bfloat16


def selections(routes, group):
    tok, topk = routes.shape
    pairs = tok * topk
    onehot = (routes.reshape(-1)[:, None] == jnp.arange(EXPERTS, dtype=jnp.int32)).astype(f32)
    earlier = (jnp.arange(pairs)[:, None] > jnp.arange(pairs)[None, :]).astype(f32)
    before = jnp.dot(earlier, onehot, preferred_element_type=f32)
    slot = jnp.sum(before * onehot, axis=1)
    span = 2 * CAPACITY
    columns = jnp.arange(EXPERTS * group * span, dtype=jnp.int32)
    expert_of = columns // (group * span)
    slot_of = (columns % span).astype(f32)
    mine = routes.reshape(-1)[:, None] == expert_of

    def at(shift):
        sel = (mine & (slot[:, None] + shift == slot_of)).astype(bf16)
        return sel.reshape(tok, topk, -1)

    first, second = at(0.0), at(float(CAPACITY))
    return [(first[:, k], second[:, k]) for k in range(topk)]


def adam_body(scale, a_ref, b_ref, w_ref, m_ref, v_ref, nw_ref, nm_ref, nv_ref):
    total = lax.dot_general(
        a_ref[...], b_ref[...], (((0,), (0,)), ((), ())), preferred_element_type=f32
    )
    grad = total * scale
    moment = first_decay * m_ref[...] + (1.0 - first_decay) * grad
    second = second_decay * v_ref[...] + (1.0 - second_decay) * grad * grad
    update = moment / first_correction / (jnp.sqrt(second / second_correction) + adam_epsilon)
    nw_ref[...] = (w_ref[...].astype(f32) - learn_rate * update).astype(bf16)
    nm_ref[...] = moment
    nv_ref[...] = second


def grad_adam(a, b, first, w, m, v, scale):
    rows = a.shape[0]
    parts, width, cols = w.shape
    tile = 128 if width % 128 == 0 else width
    state = pl.BlockSpec((None, tile, cols), lambda g, i: (g, i, 0))
    size = parts * width * cols
    return pl.pallas_call(
        functools.partial(adam_body, scale),
        grid=(parts, width // tile),
        in_specs=[
            pl.BlockSpec((rows, tile), lambda g, i: (0, i)),
            pl.BlockSpec((rows, cols), lambda g, i: (0, first + g)),
            state,
            state,
            state,
        ],
        out_specs=[state, state, state],
        out_shape=[
            jax.ShapeDtypeStruct(w.shape, bf16),
            jax.ShapeDtypeStruct(m.shape, f32),
            jax.ShapeDtypeStruct(v.shape, f32),
        ],
        compiler_params=pltpu.CompilerParams(vmem_limit_bytes=48 * 2**20),
        cost_estimate=pl.CostEstimate(
            flops=2 * rows * size, bytes_accessed=20 * size, transcendentals=2 * size
        ),
        name="grad_adam",
    )(a, b, w, m, v)


SKEW = 2


def line_body(n, chunk, count, ab_ref, g_ref, out_ref, sums, got, send, recv):
    d = lax.axis_index("dp")
    last = n - 1
    hid = g_ref.shape[1]
    half = chunk * count
    has_low, has_high = d > 0, d < last

    barrier = pltpu.get_barrier_semaphore()
    for present, peer in ((has_low, d - 1), (has_high, d + 1)):

        @pl.when(present)
        def _():
            pl.semaphore_signal(
                barrier, inc=1, device_id={"dp": peer}, device_id_type=pl.DeviceIdType.MESH
            )

    pl.semaphore_wait(barrier, has_low.astype(jnp.int32) + has_high.astype(jnp.int32))

    peers = (d + 1, d - 1)
    starts = (d == 0, d == last)
    ends = (d == last, d == 0)

    def rows_of(w, c):
        return pl.ds(pl.multiple_of(w * half + c * chunk, 16), chunk)

    def sum_copy(w, c):
        return pltpu.make_async_remote_copy(
            src_ref=sums.at[rows_of(w, c), :],
            dst_ref=got.at[rows_of(w, c), :],
            send_sem=send.at[w, c],
            recv_sem=recv.at[w, c],
            device_id={"dp": peers[w]},
            device_id_type=pl.DeviceIdType.MESH,
        )

    def result_copy(w, c):
        return pltpu.make_async_remote_copy(
            src_ref=out_ref.at[rows_of(w, c), :],
            dst_ref=out_ref.at[rows_of(w, c), :],
            send_sem=send.at[2 + w, c],
            recv_sem=recv.at[2 + w, c],
            device_id={"dp": peers[1 - w]},
            device_id_type=pl.DeviceIdType.MESH,
        )

    def step(s, carry):
        for w in range(2):
            place = d if w == 0 else last - d
            c = s - SKEW * place

            @pl.when((c >= 0) & (c < count))
            def _():
                rows = rows_of(w, c)

                @pl.when(starts[w])
                def _():
                    sums[rows, : 2 * hid] = ab_ref[rows, :]
                    sums[rows, 2 * hid :] = g_ref[rows, :]
                    sum_copy(w, c).start()

                @pl.when(jnp.logical_not(starts[w]))
                def _():
                    sum_copy(w, c).wait_recv()

                @pl.when(jnp.logical_not(starts[w] | ends[w]))
                def _():
                    sums[rows, : 2 * hid] = (
                        got[rows, : 2 * hid].astype(f32) + ab_ref[rows, :].astype(f32)
                    ).astype(bf16)
                    sums[rows, 2 * hid :] = (
                        got[rows, 2 * hid :].astype(f32) + g_ref[rows, :].astype(f32)
                    ).astype(bf16)
                    sum_copy(w, c).start()

                @pl.when(ends[w])
                def _():
                    a = got[rows, :hid].astype(f32) + ab_ref[rows, :hid].astype(f32)
                    b = got[rows, hid : 2 * hid].astype(f32) + ab_ref[rows, hid:].astype(f32)
                    g = got[rows, 2 * hid :].astype(f32) + g_ref[rows, :].astype(f32)
                    sig = jax.nn.sigmoid(a)
                    out_ref[rows, :hid] = (a * sig * b).astype(bf16)
                    out_ref[rows, hid : 2 * hid] = (
                        g * b * sig * (1.0 + a * (1.0 - sig))
                    ).astype(bf16)
                    out_ref[rows, 2 * hid :] = (g * a * sig).astype(bf16)
                    result_copy(w, c).start()

        for w in range(2):
            place = d if w == 0 else last - d
            c = s - SKEW * (2 * last - place)

            @pl.when((c >= 0) & (c < count) & jnp.logical_not(ends[w]))
            def _():
                result_copy(w, c).wait_recv()

                @pl.when(jnp.logical_not(starts[w]))
                def _():
                    result_copy(w, c).start()

        return carry

    lax.fori_loop(0, count + 2 * SKEW * last, step, 0)

    def drain(c, carry):
        for w in range(2):

            @pl.when(jnp.logical_not(ends[w]))
            def _():
                sum_copy(w, c).wait_send()

            @pl.when(jnp.logical_not(starts[w]))
            def _():
                result_copy(w, c).wait_send()

        return carry

    lax.fori_loop(0, count, drain, 0)


def line_activations(ab, g, n):
    rows, hid = g.shape
    half = rows // 2
    count = max(c for c in range(1, 21) if half % (16 * c) == 0)
    whole = pl.BlockSpec(memory_space=pltpu.VMEM)
    full = jax.ShapeDtypeStruct((rows, 3 * hid), bf16)
    return pl.pallas_call(
        functools.partial(line_body, n, half // count, count),
        out_shape=full,
        in_specs=[whole, whole],
        out_specs=whole,
        scratch_shapes=[
            pltpu.VMEM(full.shape, bf16),
            pltpu.VMEM(full.shape, bf16),
            pltpu.SemaphoreType.DMA((4, count)),
            pltpu.SemaphoreType.DMA((4, count)),
        ],
        compiler_params=pltpu.CompilerParams(
            collective_id=0, has_side_effects=True, vmem_limit_bytes=56 * 2**20
        ),
        cost_estimate=pl.CostEstimate(
            flops=30 * rows * hid, bytes_accessed=12 * rows * hid, transcendentals=rows * hid
        ),
        name="line_activations",
    )(ab, g)


def shards(
    tokens, cotangent, routes, gates, w_gate_up, w_down, m_gate_up, v_gate_up, m_down, v_down
):
    n_expert = lax.axis_size("expert")
    n_data = lax.axis_size("dp")
    group = n_expert // EXPERTS
    tok, width = tokens.shape
    topk = routes.shape[1]
    block = width // n_data
    rows = n_data * n_expert * CAPACITY
    peers = n_data * n_expert
    span = 2 * CAPACITY
    hid = w_gate_up.shape[2]
    sels = selections(routes, group)
    both = jnp.concatenate([s for pair in sels for s in pair], axis=0)

    cot = cotangent.astype(f32)
    source = []
    for k in range(topk):
        source += [tokens, (gates[:, k, None] * cot).astype(bf16)]
    packed = lax.dot_general(
        both,
        jnp.concatenate(source, axis=0),
        (((0,), (0,)), ((), ())),
        preferred_element_type=f32,
    ).astype(bf16)
    packed = jnp.stack([packed[:, d * block : (d + 1) * block] for d in range(n_data)])
    got = lax.all_to_all(
        packed.reshape(peers, span, block), BOTH, split_axis=0, concat_axis=0, tiled=True
    )
    inputs = got[:, :CAPACITY].reshape(rows, block)
    grads_in = got[:, CAPACITY:].reshape(rows, block)

    across = (((1,), (1,)), ((), ()))
    side_by_side = jnp.concatenate([w_gate_up[0], w_gate_up[1]], axis=1)
    pre = jnp.dot(inputs, side_by_side, preferred_element_type=f32).astype(bf16)
    d_hidden = lax.dot_general(grads_in, w_down, across, preferred_element_type=f32).astype(bf16)
    acts = line_activations(pre, d_hidden, n_data)

    out_part = jnp.dot(acts[:, :hid], w_down, preferred_element_type=f32).astype(bf16)
    in_part = lax.dot_general(
        acts[:, hid:], side_by_side, across, preferred_element_type=f32
    ).astype(bf16)
    parts = jnp.concatenate(
        [x.reshape(peers, CAPACITY, block) for x in (out_part, in_part)], axis=1
    )
    back = lax.all_to_all(parts, BOTH, split_axis=0, concat_axis=0, tiled=True)
    back = back.reshape(n_data, n_expert * span, block)
    outputs, input_grads = 0.0, 0.0
    for k, (first, second) in enumerate(sels):
        outs, ins = (
            jnp.concatenate(
                [jnp.dot(s, back[d], preferred_element_type=f32) for d in range(n_data)], axis=1
            )
            for s in (first, second)
        )
        outputs = outputs + gates[:, k, None] * outs
        input_grads = input_grads + ins
    outputs, input_grads = outputs.astype(bf16), input_grads.astype(bf16)

    scale = (tok * n_data * n_expert * topk / EXPERTS) ** (-0.5)
    new_wd, new_md, new_vd = (
        x[0]
        for x in grad_adam(
            acts, grads_in, 0, w_down[None], m_down[None], v_down[None], scale
        )
    )
    new_wu, new_mu, new_vu = grad_adam(inputs, acts, 1, w_gate_up, m_gate_up, v_gate_up, scale)
    return (outputs, input_grads, new_wu, new_mu, new_vu, new_wd, new_md, new_vd)


def solution(mesh):
    rows = P(BOTH, None)
    up, down = P(None, "dp", "expert"), P("expert", "dp")
    return jax.shard_map(
        shards,
        mesh=mesh,
        in_specs=(rows, rows, rows, rows, up, down, up, up, down, down),
        out_specs=(rows, rows, up, up, up, down, down, down),
        check_vma=False,
    )
```

```python
import functools

import jax
import jax.numpy as jnp
from jax import lax
from jax.experimental import pallas as pl
from jax.experimental.pallas import tpu as pltpu
from jax.sharding import PartitionSpec as P

EXPERTS = 8
CAPACITY = 20
MAIN = 16
BOTH = ("dp", "expert")

first_decay = 0.9
second_decay = 0.95
first_correction = 1.0 - 0.9**50 * 0.9**50
second_correction = 1.0 - 0.95**50 * 0.95**50
learn_rate = 0.01
adam_epsilon = 1e-08
f32, bf16 = jnp.float32, jnp.bfloat16


def selections(routes, group):
    tok, topk = routes.shape
    pairs = tok * topk
    onehot = (routes.reshape(-1)[:, None] == jnp.arange(EXPERTS, dtype=jnp.int32)).astype(f32)
    earlier = (jnp.arange(pairs)[:, None] > jnp.arange(pairs)[None, :]).astype(f32)
    before = jnp.dot(earlier, onehot, preferred_element_type=f32)
    slot = jnp.sum(before * onehot, axis=1)
    span = 2 * CAPACITY
    columns = jnp.arange(EXPERTS * group * span, dtype=jnp.int32)
    expert_of = columns // (group * span)
    slot_of = (columns % span).astype(f32)
    mine = routes.reshape(-1)[:, None] == expert_of

    def at(place):
        return (mine & (place[:, None] == slot_of)).astype(bf16).reshape(tok, topk, -1)

    first = at(jnp.where(slot < MAIN, slot, slot + MAIN))
    second = at(jnp.where(slot < MAIN, slot + MAIN, slot + CAPACITY))
    return [(first[:, k], second[:, k]) for k in range(topk)]


def adam_body(scale, a_ref, b_ref, w_ref, m_ref, v_ref, nw_ref, nm_ref, nv_ref):
    total = lax.dot_general(
        a_ref[...], b_ref[...], (((0,), (0,)), ((), ())), preferred_element_type=f32
    )
    grad = total * scale
    moment = first_decay * m_ref[...] + (1.0 - first_decay) * grad
    second = second_decay * v_ref[...] + (1.0 - second_decay) * grad * grad
    update = moment / first_correction / (jnp.sqrt(second / second_correction) + adam_epsilon)
    nw_ref[...] = (w_ref[...].astype(f32) - learn_rate * update).astype(bf16)
    nm_ref[...] = moment
    nv_ref[...] = second


def grad_adam(a, b, first, w, m, v, scale):
    rows = a.shape[1]
    parts, width, cols = w.shape
    tile = 128 if width % 128 == 0 else width
    state = pl.BlockSpec((None, tile, cols), lambda g, i: (g, i, 0))
    size = parts * width * cols
    return pl.pallas_call(
        functools.partial(adam_body, scale),
        grid=(parts, width // tile),
        in_specs=[
            pl.BlockSpec((None, rows, tile), lambda g, i: (0, 0, i)),
            pl.BlockSpec((None, rows, cols), lambda g, i: (first + g, 0, 0)),
            state,
            state,
            state,
        ],
        out_specs=[state, state, state],
        out_shape=[
            jax.ShapeDtypeStruct(w.shape, bf16),
            jax.ShapeDtypeStruct(m.shape, f32),
            jax.ShapeDtypeStruct(v.shape, f32),
        ],
        compiler_params=pltpu.CompilerParams(vmem_limit_bytes=48 * 2**20),
        cost_estimate=pl.CostEstimate(
            flops=2 * rows * size, bytes_accessed=20 * size, transcendentals=2 * size
        ),
        name="grad_adam",
    )(a, b, w, m, v)


SKEW = 2


def line_body(n, chunk, count, splits, ab_ref, g_ref, out_ref, sums, got, send, recv):
    d = lax.axis_index("dp")
    last = n - 1
    hid = g_ref.shape[1]
    half = chunk * (count // splits)
    width = hid // splits
    has_low, has_high = d > 0, d < last

    barrier = pltpu.get_barrier_semaphore()
    for present, peer in ((has_low, d - 1), (has_high, d + 1)):

        @pl.when(present)
        def _():
            pl.semaphore_signal(
                barrier, inc=1, device_id={"dp": peer}, device_id_type=pl.DeviceIdType.MESH
            )

    pl.semaphore_wait(barrier, has_low.astype(jnp.int32) + has_high.astype(jnp.int32))

    peers = (d + 1, d - 1)
    starts = (d == 0, d == last)
    ends = (d == last, d == 0)

    def rows_of(w, c):
        return pl.ds(pl.multiple_of(w * half + lax.div(c, splits) * chunk, 16), chunk)

    def columns_of(c, part):
        start = part * hid + lax.rem(c, splits) * width
        return pl.ds(pl.multiple_of(start, 128), width)

    def piece(w, c):
        return (slice(None), rows_of(w, c), columns_of(c, 0))

    def own(w, c, part):
        ref = g_ref if part == 2 else ab_ref
        return ref[rows_of(w, c), columns_of(c, part if part < 2 else 0)]

    def sum_copy(w, c):
        return pltpu.make_async_remote_copy(
            src_ref=sums.at[piece(w, c)],
            dst_ref=got.at[piece(w, c)],
            send_sem=send.at[w, c],
            recv_sem=recv.at[w, c],
            device_id={"dp": peers[w]},
            device_id_type=pl.DeviceIdType.MESH,
        )

    def result_copy(w, c):
        return pltpu.make_async_remote_copy(
            src_ref=out_ref.at[piece(w, c)],
            dst_ref=out_ref.at[piece(w, c)],
            send_sem=send.at[2 + w, c],
            recv_sem=recv.at[2 + w, c],
            device_id={"dp": peers[1 - w]},
            device_id_type=pl.DeviceIdType.MESH,
        )

    def step(s, carry):
        for w in range(2):
            place = d if w == 0 else last - d
            c = s - SKEW * place

            @pl.when((c >= 0) & (c < count))
            def _():
                rows, columns = rows_of(w, c), columns_of(c, 0)

                @pl.when(starts[w])
                def _():
                    for part in range(3):
                        sums[part, rows, columns] = own(w, c, part)
                    sum_copy(w, c).start()

                @pl.when(jnp.logical_not(starts[w]))
                def _():
                    sum_copy(w, c).wait_recv()

                @pl.when(jnp.logical_not(starts[w] | ends[w]))
                def _():
                    for part in range(3):
                        sums[part, rows, columns] = (
                            got[part, rows, columns].astype(f32) + own(w, c, part).astype(f32)
                        ).astype(bf16)
                    sum_copy(w, c).start()

                @pl.when(ends[w])
                def _():
                    a, b, g = (
                        got[part, rows, columns].astype(f32) + own(w, c, part).astype(f32)
                        for part in range(3)
                    )
                    sig = jax.nn.sigmoid(a)
                    out_ref[0, rows, columns] = (a * sig * b).astype(bf16)
                    out_ref[1, rows, columns] = (g * b * sig * (1.0 + a * (1.0 - sig))).astype(bf16)
                    out_ref[2, rows, columns] = (g * a * sig).astype(bf16)
                    result_copy(w, c).start()

        for w in range(2):
            place = d if w == 0 else last - d
            c = s - SKEW * (2 * last - place)

            @pl.when((c >= 0) & (c < count) & jnp.logical_not(ends[w]))
            def _():
                result_copy(w, c).wait_recv()

                @pl.when(jnp.logical_not(starts[w]))
                def _():
                    result_copy(w, c).start()

        return carry

    lax.fori_loop(0, count + 2 * SKEW * last, step, 0)

    def drain(c, carry):
        for w in range(2):

            @pl.when(jnp.logical_not(ends[w]))
            def _():
                sum_copy(w, c).wait_send()

            @pl.when(jnp.logical_not(starts[w]))
            def _():
                result_copy(w, c).wait_send()

        return carry

    lax.fori_loop(0, count, drain, 0)


def line_activations(ab, g, n):
    rows, hid = g.shape
    half = rows // 2
    count = max(c for c in range(1, 21) if half % (16 * c) == 0)
    chunk = half // count
    splits = 2 if hid % 256 == 0 else 1
    count = count * splits
    whole = pl.BlockSpec(memory_space=pltpu.VMEM)
    full = jax.ShapeDtypeStruct((3, rows, hid), bf16)
    return pl.pallas_call(
        functools.partial(line_body, n, chunk, count, splits),
        out_shape=full,
        in_specs=[whole, whole],
        out_specs=whole,
        scratch_shapes=[
            pltpu.VMEM(full.shape, bf16),
            pltpu.VMEM(full.shape, bf16),
            pltpu.SemaphoreType.DMA((4, count)),
            pltpu.SemaphoreType.DMA((4, count)),
        ],
        compiler_params=pltpu.CompilerParams(
            collective_id=0, has_side_effects=True, vmem_limit_bytes=56 * 2**20
        ),
        cost_estimate=pl.CostEstimate(
            flops=30 * rows * hid, bytes_accessed=12 * rows * hid, transcendentals=rows * hid
        ),
        name="line_activations",
    )(ab, g)


def shards(
    tokens, cotangent, routes, gates, w_gate_up, w_down, m_gate_up, v_gate_up, m_down, v_down
):
    n_expert = lax.axis_size("expert")
    n_data = lax.axis_size("dp")
    group = n_expert // EXPERTS
    tok, width = tokens.shape
    topk = routes.shape[1]
    block = width // n_data
    peers = n_data * n_expert
    span = 2 * CAPACITY
    sels = selections(routes, group)
    both = jnp.concatenate([s for pair in sels for s in pair], axis=0)

    cot = cotangent.astype(f32)
    source = []
    for k in range(topk):
        source += [tokens, (gates[:, k, None] * cot).astype(bf16)]
    packed = lax.dot_general(
        both,
        jnp.concatenate(source, axis=0),
        (((0,), (0,)), ((), ())),
        preferred_element_type=f32,
    ).astype(bf16)
    packed = jnp.stack([packed[:, d * block : (d + 1) * block] for d in range(n_data)])
    got = lax.all_to_all(
        packed.reshape(peers, span, block), BOTH, split_axis=0, concat_axis=0, tiled=True
    )

    def joined(main, other):
        return jnp.concatenate([main.reshape(-1, block), other.reshape(-1, block)], axis=0)

    rest = CAPACITY - MAIN
    inputs = joined(got[:, :MAIN], got[:, 2 * MAIN : 2 * MAIN + rest])
    grads_in = joined(got[:, MAIN : 2 * MAIN], got[:, 2 * MAIN + rest :])

    across = (((1,), (1,)), ((), ()))
    side_by_side = jnp.concatenate([w_gate_up[0], w_gate_up[1]], axis=1)
    pre = jnp.dot(inputs, side_by_side, preferred_element_type=f32).astype(bf16)
    d_hidden = lax.dot_general(grads_in, w_down, across, preferred_element_type=f32).astype(bf16)
    acts = line_activations(pre, d_hidden, n_data)

    out_part = jnp.dot(acts[0], w_down, preferred_element_type=f32).astype(bf16)
    in_part = lax.dot_general(
        jnp.concatenate([acts[1], acts[2]], axis=1),
        side_by_side,
        across,
        preferred_element_type=f32,
    ).astype(bf16)
    parts = jnp.concatenate(
        [x[: peers * MAIN].reshape(peers, MAIN, block) for x in (out_part, in_part)]
        + [x[peers * MAIN :].reshape(peers, rest, block) for x in (out_part, in_part)],
        axis=1,
    )
    back = lax.all_to_all(parts, BOTH, split_axis=0, concat_axis=0, tiled=True)
    back = back.reshape(n_data, n_expert * span, block)
    outputs, input_grads = 0.0, 0.0
    for k, (first, second) in enumerate(sels):
        outs, ins = (
            jnp.concatenate(
                [jnp.dot(s, back[d], preferred_element_type=f32) for d in range(n_data)], axis=1
            )
            for s in (first, second)
        )
        outputs = outputs + gates[:, k, None] * outs
        input_grads = input_grads + ins
    outputs, input_grads = outputs.astype(bf16), input_grads.astype(bf16)

    scale = (tok * n_data * n_expert * topk / EXPERTS) ** (-0.5)
    new_wd, new_md, new_vd = (
        x[0]
        for x in grad_adam(
            acts, grads_in[None], 0, w_down[None], m_down[None], v_down[None], scale
        )
    )
    new_wu, new_mu, new_vu = grad_adam(inputs[None], acts, 1, w_gate_up, m_gate_up, v_gate_up, scale)
    return (outputs, input_grads, new_wu, new_mu, new_vu, new_wd, new_md, new_vd)


def solution(mesh):
    rows = P(BOTH, None)
    up, down = P(None, "dp", "expert"), P("expert", "dp")
    return jax.shard_map(
        shards,
        mesh=mesh,
        in_specs=(rows, rows, rows, rows, up, down, up, up, down, down),
        out_specs=(rows, rows, up, up, up, down, down, down),
        check_vma=False,
    )
```

```python
import functools

import jax
import jax.numpy as jnp
from jax import lax
from jax.experimental import pallas as pl
from jax.experimental.pallas import tpu as pltpu
from jax.sharding import PartitionSpec as P

EXPERTS = 8
CAPACITY = 20
MAIN = 16
BOTH = ("dp", "expert")

first_decay = 0.9
second_decay = 0.95
first_correction = 1.0 - 0.9**50 * 0.9**50
second_correction = 1.0 - 0.95**50 * 0.95**50
learn_rate = 0.01
adam_epsilon = 1e-08
f32, bf16 = jnp.float32, jnp.bfloat16


def selections(routes, group):
    tok, topk = routes.shape
    pairs = tok * topk
    onehot = (routes.reshape(-1)[:, None] == jnp.arange(EXPERTS, dtype=jnp.int32)).astype(f32)
    earlier = (jnp.arange(pairs)[:, None] > jnp.arange(pairs)[None, :]).astype(f32)
    before = jnp.dot(earlier, onehot, preferred_element_type=f32)
    slot = jnp.sum(before * onehot, axis=1)
    span = 2 * CAPACITY
    columns = jnp.arange(EXPERTS * group * span, dtype=jnp.int32)
    expert_of = columns // (group * span)
    slot_of = (columns % span).astype(f32)
    mine = routes.reshape(-1)[:, None] == expert_of

    def at(place):
        return (mine & (place[:, None] == slot_of)).astype(bf16).reshape(tok, topk, -1)

    first = at(jnp.where(slot < MAIN, slot, slot + MAIN))
    second = at(jnp.where(slot < MAIN, slot + MAIN, slot + CAPACITY))
    return [(first[:, k], second[:, k]) for k in range(topk)]


def adam_body(scale, a_ref, b_ref, w_ref, m_ref, v_ref, nw_ref, nm_ref, nv_ref):
    total = lax.dot_general(
        a_ref[...], b_ref[...], (((0,), (0,)), ((), ())), preferred_element_type=f32
    )
    grad = total * scale
    moment = first_decay * m_ref[...] + (1.0 - first_decay) * grad
    second = second_decay * v_ref[...] + (1.0 - second_decay) * grad * grad
    update = moment / first_correction / (jnp.sqrt(second / second_correction) + adam_epsilon)
    nw_ref[...] = (w_ref[...].astype(f32) - learn_rate * update).astype(bf16)
    nm_ref[...] = moment
    nv_ref[...] = second


def grad_adam(a, b, first, w, m, v, scale):
    rows = a.shape[1]
    parts, width, cols = w.shape
    tile = 128 if width % 128 == 0 else width
    state = pl.BlockSpec((None, tile, cols), lambda g, i: (g, i, 0))
    size = parts * width * cols
    return pl.pallas_call(
        functools.partial(adam_body, scale),
        grid=(parts, width // tile),
        in_specs=[
            pl.BlockSpec((None, rows, tile), lambda g, i: (0, 0, i)),
            pl.BlockSpec((None, rows, cols), lambda g, i: (first + g, 0, 0)),
            state,
            state,
            state,
        ],
        out_specs=[state, state, state],
        out_shape=[
            jax.ShapeDtypeStruct(w.shape, bf16),
            jax.ShapeDtypeStruct(m.shape, f32),
            jax.ShapeDtypeStruct(v.shape, f32),
        ],
        compiler_params=pltpu.CompilerParams(vmem_limit_bytes=48 * 2**20),
        cost_estimate=pl.CostEstimate(
            flops=2 * rows * size, bytes_accessed=20 * size, transcendentals=2 * size
        ),
        name="grad_adam",
    )(a, b, w, m, v)


SKEW = 1


def line_body(n, chunk, count, splits, ab_ref, g_ref, out_ref, sums, got, send, recv):
    d = lax.axis_index("dp")
    last = n - 1
    hid = g_ref.shape[1]
    half = chunk * (count // splits)
    width = hid // splits
    has_low, has_high = d > 0, d < last

    barrier = pltpu.get_barrier_semaphore()
    for present, peer in ((has_low, d - 1), (has_high, d + 1)):

        @pl.when(present)
        def _():
            pl.semaphore_signal(
                barrier, inc=1, device_id={"dp": peer}, device_id_type=pl.DeviceIdType.MESH
            )

    pl.semaphore_wait(barrier, has_low.astype(jnp.int32) + has_high.astype(jnp.int32))

    peers = (d + 1, d - 1)
    starts = (d == 0, d == last)
    ends = (d == last, d == 0)

    def rows_of(w, c):
        return pl.ds(pl.multiple_of(w * half + lax.div(c, splits) * chunk, 16), chunk)

    def columns_of(c, part):
        start = part * hid + lax.rem(c, splits) * width
        return pl.ds(pl.multiple_of(start, 128), width)

    def piece(w, c):
        return (slice(None), rows_of(w, c), columns_of(c, 0))

    def own(w, c, part):
        ref = g_ref if part == 2 else ab_ref
        return ref[rows_of(w, c), columns_of(c, part if part < 2 else 0)]

    def sum_copy(w, c):
        return pltpu.make_async_remote_copy(
            src_ref=sums.at[piece(w, c)],
            dst_ref=got.at[piece(w, c)],
            send_sem=send.at[w, c],
            recv_sem=recv.at[w, c],
            device_id={"dp": peers[w]},
            device_id_type=pl.DeviceIdType.MESH,
        )

    def result_copy(w, c):
        return pltpu.make_async_remote_copy(
            src_ref=out_ref.at[piece(w, c)],
            dst_ref=out_ref.at[piece(w, c)],
            send_sem=send.at[2 + w, c],
            recv_sem=recv.at[2 + w, c],
            device_id={"dp": peers[1 - w]},
            device_id_type=pl.DeviceIdType.MESH,
        )

    def step(s, carry):
        for w in range(2):
            place = d if w == 0 else last - d
            c = s - SKEW * place

            @pl.when((c >= 0) & (c < count))
            def _():
                rows, columns = rows_of(w, c), columns_of(c, 0)

                @pl.when(starts[w])
                def _():
                    for part in range(3):
                        sums[part, rows, columns] = own(w, c, part)
                    sum_copy(w, c).start()

                @pl.when(jnp.logical_not(starts[w]))
                def _():
                    sum_copy(w, c).wait_recv()

                @pl.when(jnp.logical_not(starts[w] | ends[w]))
                def _():
                    for part in range(3):
                        sums[part, rows, columns] = (
                            got[part, rows, columns].astype(f32) + own(w, c, part).astype(f32)
                        ).astype(bf16)
                    sum_copy(w, c).start()

                @pl.when(ends[w])
                def _():
                    a, b, g = (
                        got[part, rows, columns].astype(f32) + own(w, c, part).astype(f32)
                        for part in range(3)
                    )
                    sig = jax.nn.sigmoid(a)
                    out_ref[0, rows, columns] = (a * sig * b).astype(bf16)
                    out_ref[1, rows, columns] = (g * b * sig * (1.0 + a * (1.0 - sig))).astype(bf16)
                    out_ref[2, rows, columns] = (g * a * sig).astype(bf16)
                    result_copy(w, c).start()

        for w in range(2):
            place = d if w == 0 else last - d
            c = s - SKEW * (2 * last - place)

            @pl.when((c >= 0) & (c < count) & jnp.logical_not(ends[w]))
            def _():
                result_copy(w, c).wait_recv()

                @pl.when(jnp.logical_not(starts[w]))
                def _():
                    result_copy(w, c).start()

        return carry

    lax.fori_loop(0, count + 2 * SKEW * last, step, 0)

    def drain(c, carry):
        for w in range(2):

            @pl.when(jnp.logical_not(ends[w]))
            def _():
                sum_copy(w, c).wait_send()

            @pl.when(jnp.logical_not(starts[w]))
            def _():
                result_copy(w, c).wait_send()

        return carry

    lax.fori_loop(0, count, drain, 0)


def line_activations(ab, g, n):
    rows, hid = g.shape
    half = rows // 2
    count = max(c for c in range(1, 21) if half % (16 * c) == 0)
    chunk = half // count
    splits = 2 if hid % 256 == 0 else 1
    count = count * splits
    whole = pl.BlockSpec(memory_space=pltpu.VMEM)
    full = jax.ShapeDtypeStruct((3, rows, hid), bf16)
    return pl.pallas_call(
        functools.partial(line_body, n, chunk, count, splits),
        out_shape=full,
        in_specs=[whole, whole],
        out_specs=whole,
        scratch_shapes=[
            pltpu.VMEM(full.shape, bf16),
            pltpu.VMEM(full.shape, bf16),
            pltpu.SemaphoreType.DMA((4, count)),
            pltpu.SemaphoreType.DMA((4, count)),
        ],
        compiler_params=pltpu.CompilerParams(
            collective_id=0, has_side_effects=True, vmem_limit_bytes=56 * 2**20
        ),
        cost_estimate=pl.CostEstimate(
            flops=30 * rows * hid, bytes_accessed=12 * rows * hid, transcendentals=rows * hid
        ),
        name="line_activations",
    )(ab, g)


def shards(
    tokens, cotangent, routes, gates, w_gate_up, w_down, m_gate_up, v_gate_up, m_down, v_down
):
    n_expert = lax.axis_size("expert")
    n_data = lax.axis_size("dp")
    group = n_expert // EXPERTS
    tok, width = tokens.shape
    topk = routes.shape[1]
    block = width // n_data
    peers = n_data * n_expert
    span = 2 * CAPACITY
    sels = selections(routes, group)
    both = jnp.concatenate([s for pair in sels for s in pair], axis=0)

    cot = cotangent.astype(f32)
    source = []
    for k in range(topk):
        source += [tokens, (gates[:, k, None] * cot).astype(bf16)]
    packed = lax.dot_general(
        both,
        jnp.concatenate(source, axis=0),
        (((0,), (0,)), ((), ())),
        preferred_element_type=f32,
    ).astype(bf16)
    packed = jnp.stack([packed[:, d * block : (d + 1) * block] for d in range(n_data)])
    got = lax.all_to_all(
        packed.reshape(peers, span, block), BOTH, split_axis=0, concat_axis=0, tiled=True
    )

    def joined(main, other):
        return jnp.concatenate([main.reshape(-1, block), other.reshape(-1, block)], axis=0)

    rest = CAPACITY - MAIN
    inputs = joined(got[:, :MAIN], got[:, 2 * MAIN : 2 * MAIN + rest])
    grads_in = joined(got[:, MAIN : 2 * MAIN], got[:, 2 * MAIN + rest :])

    across = (((1,), (1,)), ((), ()))
    side_by_side = jnp.concatenate([w_gate_up[0], w_gate_up[1]], axis=1)
    pre = jnp.dot(inputs, side_by_side, preferred_element_type=f32).astype(bf16)
    d_hidden = lax.dot_general(grads_in, w_down, across, preferred_element_type=f32).astype(bf16)
    acts = line_activations(pre, d_hidden, n_data)

    out_part = jnp.dot(acts[0], w_down, preferred_element_type=f32).astype(bf16)
    in_part = lax.dot_general(
        jnp.concatenate([acts[1], acts[2]], axis=1),
        side_by_side,
        across,
        preferred_element_type=f32,
    ).astype(bf16)
    parts = jnp.concatenate(
        [x[: peers * MAIN].reshape(peers, MAIN, block) for x in (out_part, in_part)]
        + [x[peers * MAIN :].reshape(peers, rest, block) for x in (out_part, in_part)],
        axis=1,
    )
    back = lax.all_to_all(parts, BOTH, split_axis=0, concat_axis=0, tiled=True)
    back = back.reshape(n_data, n_expert * span, block)
    outputs, input_grads = 0.0, 0.0
    for k, (first, second) in enumerate(sels):
        outs, ins = (
            jnp.concatenate(
                [jnp.dot(s, back[d], preferred_element_type=f32) for d in range(n_data)], axis=1
            )
            for s in (first, second)
        )
        outputs = outputs + gates[:, k, None] * outs
        input_grads = input_grads + ins
    outputs, input_grads = outputs.astype(bf16), input_grads.astype(bf16)

    scale = (tok * n_data * n_expert * topk / EXPERTS) ** (-0.5)
    new_wd, new_md, new_vd = (
        x[0]
        for x in grad_adam(
            acts, grads_in[None], 0, w_down[None], m_down[None], v_down[None], scale
        )
    )
    new_wu, new_mu, new_vu = grad_adam(inputs[None], acts, 1, w_gate_up, m_gate_up, v_gate_up, scale)
    return (outputs, input_grads, new_wu, new_mu, new_vu, new_wd, new_md, new_vd)


def solution(mesh):
    rows = P(BOTH, None)
    up, down = P(None, "dp", "expert"), P("expert", "dp")
    return jax.shard_map(
        shards,
        mesh=mesh,
        in_specs=(rows, rows, rows, rows, up, down, up, up, down, down),
        out_specs=(rows, rows, up, up, up, down, down, down),
        check_vma=False,
    )
```
